128 devices in a mesh: dp: 16 (over x, z_lo, core), tensor: 8 (over z_hi, y).
Axes of the slice: x: 4, y: 4, z: 4 (z_hi: 2, z_lo: 2; z = z_hi * 2 + z_lo), core: 2. Of those that a mesh axis runs over, the one named last changes fastest.
Arguments:
- act_mant: int32 [16384, 6144], P(('dp', 'tensor')), may hold values from -127 to 127
- act_exp: int32 [16384, 48], P(('dp', 'tensor')), may hold values from -9 to -6
- grad_mant: int32 [16384, 8192], P('dp', 'tensor'), may hold values from -127 to 127
- grad_exp: int32 [128, 8192], P('dp', 'tensor'), may hold values from -14 to -11
Outputs:
- weight_grad: float32 [6144, 8192], P('dp', 'tensor')
The draws below stay inside these ranges and needn't reach their ends.
All inputs are finite; a program needn't handle non-finite values.
Results may differ from the reference program's by a relative error of at most 0.0003.
Values may be sent and summed in bfloat16 or wider, within the bound.
No kernel may reach another device: no remote copies, remote signals or barrier semaphores. Data moves between devices by JAX's collectives and lax.ppermute only.
A program may use at most 128 MiB of HBM per device.

```python
import jax
import jax.numpy as jnp
from jax import lax

D = 6144
QCOLS = 8192
GROUP = 1024
TOKENS = 16384
N_DP = 16


def set_ends(result, stream_key, low, top_value):
    index_at = [jax.random.randint(jax.random.fold_in(stream_key, axis), (), 0, length) for axis, length in enumerate(result.shape)]
    main_axis = result.shape.index(max(result.shape))
    next_to = index_at[:main_axis] + [(index_at[main_axis] + 1) % result.shape[main_axis]] + index_at[main_axis + 1:]
    return result.at[tuple(index_at)].set(low).at[tuple(next_to)].set(top_value)


def setup_inputs(seed: int = 0) -> dict:
    streams_of = jax.random.split(jax.random.key(seed), 5)
    act_mant = set_ends(jax.random.randint(streams_of[0], (TOKENS, D), -127, 128), jax.random.fold_in(streams_of[0], 1), -127, 127).astype(jnp.int32)
    act_exp = set_ends(jax.random.randint(streams_of[1], (TOKENS, D // 128), -9, -5), jax.random.fold_in(streams_of[1], 1), -9, (-5) - 1).astype(jnp.int32)
    grad_mant = set_ends(jax.random.randint(streams_of[2], (TOKENS, QCOLS), -127, 128), jax.random.fold_in(streams_of[2], 1), -127, 127).astype(jnp.int32)
    grad_exp = set_ends(jax.random.randint(streams_of[3], (TOKENS // 128, QCOLS), -14, -10), jax.random.fold_in(streams_of[3], 1), -14, (-10) - 1).astype(jnp.int32)
    return dict(act_mant=act_mant, act_exp=act_exp, grad_mant=grad_mant, grad_exp=grad_exp)


def widen_rows(mantissa, exponent):
    scale = jnp.exp2(exponent.astype(jnp.float32))
    count = mantissa.shape[0]
    blocks = exponent.shape[1]
    values = mantissa.astype(jnp.float32).reshape(count, blocks, 128) * scale[:, :, None]
    return values.reshape(count, blocks * 128).astype(jnp.bfloat16)


def widen_columns(mantissa, exponent):
    scale = jnp.exp2(exponent.astype(jnp.float32))
    blocks = exponent.shape[0]
    width = exponent.shape[1]
    values = mantissa.astype(jnp.float32).reshape(blocks, 128, width) * scale[:, None, :]
    return values.reshape(blocks * 128, width).astype(jnp.bfloat16)


def reference(act_mant, act_exp, grad_mant, grad_exp):
    act_groups = act_mant.reshape(N_DP, GROUP, D)
    act_scales = act_exp.reshape(N_DP, GROUP, D // 128)
    grad_groups = grad_mant.reshape(N_DP, GROUP, QCOLS)
    grad_scales = grad_exp.reshape(N_DP, GROUP // 128, QCOLS)

    def replica_step(running, inputs):
        act_rows, act_block, grad_rows, grad_block = inputs
        act_vals = widen_rows(act_rows, act_block)
        grad_vals = widen_columns(grad_rows, grad_block)
        replica_part = lax.dot_general(act_vals, grad_vals, (((0,), (0,)), ((), ())), preferred_element_type=jnp.float32)
        return running + replica_part, None

    initial = jnp.zeros((D, QCOLS), jnp.float32)
    weight_grad, unused = lax.scan(replica_step, initial, (act_groups, act_scales, grad_groups, grad_scales))
    return weight_grad
```

```python
import jax
import jax.numpy as jnp
from jax import lax
from jax.experimental import pallas as pl
from jax.experimental.pallas import tpu as pltpu
from jax.sharding import PartitionSpec as P

AXES = ("dp", "tensor")
BLOCK = 128
PARTS = 3


def place(index):
    dp, tensor = index // 8, index % 8
    return dp // 4, tensor % 4, (tensor // 4) * 2 + (dp // 2) % 2, dp % 2


def index_of(x, y, z, core):
    return ((x * 2 + z % 2) * 2 + core) * 8 + (z // 2) * 4 + y


def send(value, x=0, y=0, z=0, core=0):
    pairs = []
    for source in range(128):
        sx, sy, sz, sc = place(source)
        pairs.append((source, index_of((sx + x) % 4, (sy + y) % 4, sz ^ z, sc ^ core)))
    return lax.ppermute(value, AXES, pairs)


def act_kernel(where, mant, scale, out):
    x, z_lo, core = where[0], where[1], where[2]
    for owner in range(16):
        ox, oz, oc = owner // 4, (owner // 2) % 2, owner % 2
        slot = lax.rem(ox - x + 4, 4)
        for k in range(PARTS):
            b = owner * PARTS + k
            values = mant[:, b * BLOCK : (b + 1) * BLOCK].astype(jnp.float32) * scale[:, b : b + 1]
            lanes = pl.ds(pl.multiple_of(slot * BLOCK, BLOCK), BLOCK)
            out[oc ^ core, oz ^ z_lo, k, :, lanes] = values.astype(jnp.bfloat16)


def widen_act(mant, exponent, where):
    tokens = mant.shape[0]
    return pl.pallas_call(
        act_kernel,
        out_shape=jax.ShapeDtypeStruct((2, 2, PARTS, tokens, 4 * BLOCK), jnp.bfloat16),
        in_specs=[
            pl.BlockSpec(memory_space=pltpu.SMEM),
            pl.BlockSpec(memory_space=pltpu.VMEM),
            pl.BlockSpec(memory_space=pltpu.VMEM),
        ],
        out_specs=pl.BlockSpec(memory_space=pltpu.VMEM),
        compiler_params=pltpu.CompilerParams(vmem_limit_bytes=32 * 1024 * 1024),
    )(where, mant, jnp.exp2(exponent.astype(jnp.float32)))


def grad_kernel(order, mant, scale, out):
    out[0] = (mant[...].astype(jnp.float32) * scale[0]).astype(jnp.bfloat16)


def widen_grad(mant, exponent, order):
    blocks, width = exponent.shape
    scale = jnp.exp2(exponent.astype(jnp.float32)).reshape(blocks, 1, width)
    return pl.pallas_call(
        grad_kernel,
        out_shape=jax.ShapeDtypeStruct((blocks, BLOCK, width), jnp.bfloat16),
        grid_spec=pltpu.PrefetchScalarGridSpec(
            num_scalar_prefetch=1,
            grid=(blocks,),
            in_specs=[
                pl.BlockSpec((BLOCK, width), lambda i, order: (order[i], 0)),
                pl.BlockSpec((1, 1, width), lambda i, order: (order[i], 0, 0)),
            ],
            out_specs=pl.BlockSpec((1, BLOCK, width), lambda i, order: (i, 0, 0)),
        ),
        compiler_params=pltpu.CompilerParams(vmem_limit_bytes=32 * 1024 * 1024),
    )(order, mant, scale)


def contract(left, right):
    return lax.dot_general(
        left, right, (((0,), (0,)), ((), ())), preferred_element_type=jnp.float32
    )


def body(act_mant, act_exp, grad_mant, grad_exp):
    dp, tensor = lax.axis_index("dp"), lax.axis_index("tensor")
    x, z_lo, core = dp // 4, (dp // 2) % 2, dp % 2
    z_hi, y = tensor // 4, tensor % 4

    act = widen_act(act_mant, act_exp, jnp.stack([x, z_lo, core]).astype(jnp.int32))
    order = jnp.stack(
        [(z_hi ^ flip) * 4 + (y + step) % 4 for step in range(4) for flip in range(2)]
    ).astype(jnp.int32)
    own_grad = widen_grad(grad_mant, grad_exp, order).reshape(4, 2, BLOCK, -1)

    other = send(act[1], core=1)
    grad_c = send(own_grad, core=1)
    grad_z = send(own_grad, z=1)
    grad_zc = send(grad_z, core=1)
    grads = jnp.stack(
        [
            jnp.stack([own_grad, grad_c], axis=2),
            jnp.stack([grad_z, grad_zc], axis=2),
        ],
        axis=1,
    ).reshape(4, 8 * BLOCK, -1)

    width = grads.shape[-1]
    half = width // 2
    rows = []
    for k in range(PARTS):
        here, there = (
            jnp.concatenate([act[0, flip, k], other[flip, k]], axis=0) for flip in range(2)
        )
        piece = jnp.concatenate(
            [here, send(here, z=2), send(there, z=1), send(there, z=3)], axis=0
        )
        mid = piece.shape[0] // 2
        behind = send(piece, y=1)
        ahead = send(piece, y=3)
        far = jnp.concatenate([send(behind[:mid], y=1), send(ahead[mid:], y=3)], axis=0)
        total = contract(piece, grads[0]) + contract(ahead, grads[1])
        total = total + contract(behind, grads[3]) + contract(far, grads[2])
        total = total.reshape(4, BLOCK, width)
        first = send(total[2, :, :half], x=1)
        second = send(total[2, :, half:], x=3)
        to_next = jnp.concatenate([total[1, :, :half] + first, total[1, :, half:]], axis=1)
        to_last = jnp.concatenate([total[3, :, :half], total[3, :, half:] + second], axis=1)
        rows.append(total[0] + send(to_next, x=1) + send(to_last, x=3))
    return jnp.concatenate(rows, axis=0)


def solution(mesh):
    return jax.shard_map(
        body,
        mesh=mesh,
        in_specs=(
            P(("dp", "tensor"), None),
            P(("dp", "tensor"), None),
            P("dp", "tensor"),
            P("dp", "tensor"),
        ),
        out_specs=P("dp", "tensor"),
        check_vma=False,
    )
```

```python
import jax
import jax.numpy as jnp
from jax import lax
from jax.experimental import pallas as pl
from jax.experimental.pallas import tpu as pltpu
from jax.sharding import PartitionSpec as P

AXES = ("dp", "tensor")
BLOCK = 128
PARTS = 3


def place(index):
    dp, tensor = index // 8, index % 8
    return dp // 4, tensor % 4, (tensor // 4) * 2 + (dp // 2) % 2, dp % 2


def index_of(x, y, z, core):
    return ((x * 2 + z % 2) * 2 + core) * 8 + (z // 2) * 4 + y


def send(value, x=0, y=0, z=0, core=0):
    pairs = []
    for source in range(128):
        sx, sy, sz, sc = place(source)
        pairs.append((source, index_of((sx + x) % 4, (sy + y) % 4, sz ^ z, sc ^ core)))
    return lax.ppermute(value, AXES, pairs)


def act_kernel(where, mant, scale, out):
    x, z_lo, core = where[0], where[1], where[2]
    for owner in range(16):
        ox, oz, oc = owner // 4, (owner // 2) % 2, owner % 2
        slot = lax.rem(ox - x + 4, 4)
        for k in range(PARTS):
            b = owner * PARTS + k
            values = mant[:, b * BLOCK : (b + 1) * BLOCK].astype(jnp.float32) * scale[:, b : b + 1]
            lanes = pl.ds(pl.multiple_of(slot * BLOCK, BLOCK), BLOCK)
            out[oc ^ core, oz ^ z_lo, k, :, lanes] = values.astype(jnp.bfloat16)


def widen_act(mant, exponent, where):
    tokens = mant.shape[0]
    return pl.pallas_call(
        act_kernel,
        out_shape=jax.ShapeDtypeStruct((2, 2, PARTS, tokens, 4 * BLOCK), jnp.bfloat16),
        in_specs=[
            pl.BlockSpec(memory_space=pltpu.SMEM),
            pl.BlockSpec(memory_space=pltpu.VMEM),
            pl.BlockSpec(memory_space=pltpu.VMEM),
        ],
        out_specs=pl.BlockSpec(memory_space=pltpu.VMEM),
        compiler_params=pltpu.CompilerParams(vmem_limit_bytes=8 * 1024 * 1024),
        cost_estimate=pl.CostEstimate(flops=0, bytes_accessed=8 * 1024 * 1024, transcendentals=0),
    )(where, mant, jnp.exp2(exponent.astype(jnp.float32)))


def grad_kernel(order, mant, scale, out):
    out[0] = (mant[...].astype(jnp.float32) * scale[0]).astype(jnp.bfloat16)


def widen_grad(mant, exponent, order):
    blocks, width = exponent.shape
    scale = jnp.exp2(exponent.astype(jnp.float32)).reshape(blocks, 1, width)
    return pl.pallas_call(
        grad_kernel,
        out_shape=jax.ShapeDtypeStruct((blocks, BLOCK, width), jnp.bfloat16),
        grid_spec=pltpu.PrefetchScalarGridSpec(
            num_scalar_prefetch=1,
            grid=(blocks,),
            in_specs=[
                pl.BlockSpec((BLOCK, width), lambda i, order: (order[i], 0)),
                pl.BlockSpec((1, 1, width), lambda i, order: (order[i], 0, 0)),
            ],
            out_specs=pl.BlockSpec((1, BLOCK, width), lambda i, order: (i, 0, 0)),
        ),
        compiler_params=pltpu.CompilerParams(vmem_limit_bytes=8 * 1024 * 1024),
        cost_estimate=pl.CostEstimate(flops=0, bytes_accessed=16 * 1024 * 1024, transcendentals=0),
    )(order, mant, scale)


def contract(left, right):
    return lax.dot_general(
        left, right, (((0,), (0,)), ((), ())), preferred_element_type=jnp.float32
    )


Z_PAIRS = [[base, base + 2] for base in range(16) if base % 4 < 2]


def tied(values, *others):
    return lax.optimization_barrier((*values, *others))[: len(values)]


def body(act_mant, act_exp, grad_mant, grad_exp):
    dp, tensor = lax.axis_index("dp"), lax.axis_index("tensor")
    x, z_lo, core = dp // 4, (dp // 2) % 2, dp % 2
    z_hi, y = tensor // 4, tensor % 4

    act = widen_act(act_mant, act_exp, jnp.stack([x, z_lo, core]).astype(jnp.int32))
    order = jnp.stack(
        [(z_hi ^ flip) * 4 + (y + step) % 4 for step in range(4) for flip in range(2)]
    ).astype(jnp.int32)
    other = send(act[1], core=1)
    (grad_mant,) = tied((grad_mant,), act)
    own_grad = widen_grad(grad_mant, grad_exp, order).reshape(4, 2, BLOCK, -1)
    width = own_grad.shape[-1]
    half = width // 2

    def halves(k):
        return [jnp.concatenate([act[0, flip, k], other[flip, k]], axis=0) for flip in range(2)]

    def along_z(here, there):
        return [here, send(here, z=2), send(there, z=1), send(there, z=3)]

    def around_y(piece):
        return send(piece, y=1), send(piece, y=3)

    def onward_y(behind, ahead):
        mid = behind.shape[0] // 2
        return send(behind[:mid], y=1), send(ahead[mid:], y=3)

    def partial(piece, ahead, behind):
        return contract(piece, grads[0]) + contract(ahead, grads[1]) + contract(behind, grads[3])

    def finish(total, far):
        return (total + contract(jnp.concatenate(far, axis=0), grads[2])).reshape(4, BLOCK, width)

    def first_x(total):
        return send(total[2, :, :half], x=1), send(total[2, :, half:], x=3)

    def second_x(total, first, second):
        to_next = jnp.concatenate([total[1, :, :half] + first, total[1, :, half:]], axis=1)
        to_last = jnp.concatenate([total[3, :, :half], total[3, :, half:] + second], axis=1)
        return send(to_next, x=1), send(to_last, x=3)

    half0, half1, half2 = halves(0), halves(1), halves(2)
    z0 = along_z(*half0)
    (for_core,) = tied((own_grad,), other)
    grad_c = send(for_core, core=1)
    piece0 = jnp.concatenate(z0, axis=0)
    z1 = along_z(*tied(half1, piece0))
    behind0, ahead0 = around_y(piece0)
    piece1 = jnp.concatenate(z1, axis=0)
    (for_z,) = tied((own_grad,), piece1)
    grad_z = send(for_z, z=1)

    behind0, ahead0, piece1 = tied((behind0, ahead0, piece1), grad_c)
    far0 = onward_y(behind0, ahead0)
    behind1, ahead1 = around_y(piece1)
    z2 = along_z(*tied(half2, *far0))
    piece2 = jnp.concatenate(z2, axis=0)
    behind1, ahead1, piece2 = tied((behind1, ahead1, piece2))
    far1 = onward_y(behind1, ahead1)
    behind2, ahead2 = around_y(piece2)

    (for_zc,) = tied((grad_z,), behind1)
    grad_zc = send(for_zc, core=1)
    grads = jnp.stack(
        [jnp.stack([own_grad, grad_c], axis=2), jnp.stack([grad_z, grad_zc], axis=2)], axis=1
    ).reshape(4, 8 * BLOCK, width)

    total0 = finish(partial(piece0, ahead0, behind0), far0)
    total0, *far1 = tied((total0, *far1))
    x0 = first_x(total0)
    part1 = partial(piece1, ahead1, behind1)
    behind2, ahead2, part1, *x0 = tied((behind2, ahead2, part1, *x0))
    far2 = onward_y(behind2, ahead2)
    w0 = second_x(total0, *x0)
    total1 = finish(part1, far1)
    part2 = partial(piece2, ahead2, behind2)
    x1 = first_x(total1)
    part2, total1, *w0 = tied((part2, total1, *w0))
    part2, *far2 = tied((part2, *far2), *x1)
    total2 = finish(part2, far2)
    w1 = second_x(total1, *x1)
    x2 = first_x(total2)
    w2 = second_x(total2, *x2)
    rows = [total[0] + w[0] + w[1] for total, w in ((total0, w0), (total1, w1), (total2, w2))]
    return jnp.concatenate(rows, axis=0)


def solution(mesh):
    return jax.shard_map(
        body,
        mesh=mesh,
        in_specs=(
            P(("dp", "tensor"), None),
            P(("dp", "tensor"), None),
            P("dp", "tensor"),
            P("dp", "tensor"),
        ),
        out_specs=P("dp", "tensor"),
        check_vma=False,
    )
```

```python
import jax
import jax.numpy as jnp
from jax import lax
from jax.experimental import pallas as pl
from jax.experimental.pallas import tpu as pltpu
from jax.sharding import PartitionSpec as P

AXES = ("dp", "tensor")
BLOCK = 128
PARTS = 3


def place(index):
    dp, tensor = index // 8, index % 8
    return dp // 4, tensor % 4, (tensor // 4) * 2 + (dp // 2) % 2, dp % 2


def index_of(x, y, z, core):
    return ((x * 2 + z % 2) * 2 + core) * 8 + (z // 2) * 4 + y


def send(value, x=0, y=0, z=0, core=0):
    pairs = []
    for source in range(128):
        sx, sy, sz, sc = place(source)
        pairs.append((source, index_of((sx + x) % 4, (sy + y) % 4, sz ^ z, sc ^ core)))
    return lax.ppermute(value, AXES, pairs)


def act_kernel(where, mant, scale, out):
    x, z_lo, core = where[0], where[1], where[2]
    for owner in range(16):
        ox, oz, oc = owner // 4, (owner // 2) % 2, owner % 2
        slot = lax.rem(ox - x + 4, 4)
        for k in range(PARTS):
            b = owner * PARTS + k
            values = mant[:, b * BLOCK : (b + 1) * BLOCK].astype(jnp.float32) * scale[:, b : b + 1]
            lanes = pl.ds(pl.multiple_of(slot * BLOCK, BLOCK), BLOCK)
            out[oc ^ core, oz ^ z_lo, k, :, lanes] = values.astype(jnp.bfloat16)


def widen_act(mant, exponent, where):
    tokens = mant.shape[0]
    return pl.pallas_call(
        act_kernel,
        out_shape=jax.ShapeDtypeStruct((2, 2, PARTS, tokens, 4 * BLOCK), jnp.bfloat16),
        in_specs=[
            pl.BlockSpec(memory_space=pltpu.SMEM),
            pl.BlockSpec(memory_space=pltpu.VMEM),
            pl.BlockSpec(memory_space=pltpu.VMEM),
        ],
        out_specs=pl.BlockSpec(memory_space=pltpu.VMEM),
        compiler_params=pltpu.CompilerParams(vmem_limit_bytes=8 * 1024 * 1024),
        cost_estimate=pl.CostEstimate(flops=0, bytes_accessed=8 * 1024 * 1024, transcendentals=0),
    )(where, mant, jnp.exp2(exponent.astype(jnp.float32)))


def grad_kernel(order, mant, scale, out):
    out[0] = (mant[...].astype(jnp.float32) * scale[0]).astype(jnp.bfloat16)


def widen_grad(mant, exponent, order):
    blocks, width = exponent.shape
    scale = jnp.exp2(exponent.astype(jnp.float32)).reshape(blocks, 1, width)
    return pl.pallas_call(
        grad_kernel,
        out_shape=jax.ShapeDtypeStruct((blocks, BLOCK, width), jnp.bfloat16),
        grid_spec=pltpu.PrefetchScalarGridSpec(
            num_scalar_prefetch=1,
            grid=(blocks,),
            in_specs=[
                pl.BlockSpec((BLOCK, width), lambda i, order: (order[i], 0)),
                pl.BlockSpec((1, 1, width), lambda i, order: (order[i], 0, 0)),
            ],
            out_specs=pl.BlockSpec((1, BLOCK, width), lambda i, order: (i, 0, 0)),
        ),
        compiler_params=pltpu.CompilerParams(vmem_limit_bytes=8 * 1024 * 1024),
        cost_estimate=pl.CostEstimate(flops=0, bytes_accessed=16 * 1024 * 1024, transcendentals=0),
    )(order, mant, scale)


def contract(left, right):
    return lax.dot_general(
        left, right, (((0,), (0,)), ((), ())), preferred_element_type=jnp.float32
    )


def tied(values, *others):
    return lax.optimization_barrier((*values, *others))[: len(values)]


def body(act_mant, act_exp, grad_mant, grad_exp):
    dp, tensor = lax.axis_index("dp"), lax.axis_index("tensor")
    x, z_lo, core = dp // 4, (dp // 2) % 2, dp % 2
    z_hi, y = tensor // 4, tensor % 4

    act = widen_act(act_mant, act_exp, jnp.stack([x, z_lo, core]).astype(jnp.int32))
    order = jnp.stack(
        [(z_hi ^ flip) * 4 + (y + step) % 4 for step in range(4) for flip in range(2)]
    ).astype(jnp.int32)
    other = send(act[1], core=1)
    (grad_mant,) = tied((grad_mant,), act)
    own = widen_grad(grad_mant, grad_exp, order).reshape(4, 2, BLOCK, -1)
    width = own.shape[-1]
    half = width // 2
    tokens = 4 * BLOCK

    def joined(first, second):
        return jnp.stack([first, second], axis=2).reshape(4, tokens, width)

    def first_x(total):
        return send(total[..., 2, :, :half], x=1), send(total[..., 2, :, half:], x=3)

    def second_x(total, first, second):
        up, down = total[..., 1, :, :], total[..., 3, :, :]
        up = jnp.concatenate([up[..., :half] + first, up[..., half:]], axis=-1)
        down = jnp.concatenate([down[..., :half], down[..., half:] + second], axis=-1)
        return send(up, x=1), send(down, x=3)

    pair = jnp.concatenate([act[0, :, 0], other[:, 0]], axis=1)
    (for_core,) = tied((own,), other)
    piece0 = jnp.concatenate([pair, send(pair, z=2)], axis=1)
    own_c = send(for_core, core=1)
    piece0, mine, other = tied((piece0, act[0], other), own_c)
    behind0, ahead0 = send(piece0, y=1), send(piece0, y=3)
    pairs = jnp.concatenate([mine[:, 1:], other[:, 1:]], axis=2)
    here, there = pairs[0], pairs[1]
    pieces = jnp.concatenate(
        [here, send(here, z=2), send(there, z=1), send(there, z=3)], axis=1
    )
    behind0, ahead0, pieces, for_z = tied((behind0, ahead0, pieces, own))
    far0 = [send(behind0[0], y=1), send(ahead0[1], y=3)]
    near = [send(for_z[:1], z=1)]
    piece1, for_z, *far0 = tied((pieces[0], for_z, *far0, *near))[:4]
    near.append(send(for_z[1:], z=1))
    behind1, ahead1 = send(piece1, y=1), send(piece1, y=3)

    grads = joined(own, own_c)

    def with_own(steps):
        total = contract(steps[0], grads[0])
        for step in range(1, 4):
            if steps[step] is not None:
                total = total + contract(steps[step], grads[step])
        return total

    total0 = jnp.stack(
        [with_own([piece0[i], ahead0[i], far0[i], behind0[i]]) for i in range(2)]
    ).reshape(2, 4, BLOCK, width)
    x0 = first_x(total0)
    w0 = second_x(total0, *x0)
    behind1, ahead1 = tied((behind1, ahead1), *x0)
    far1 = [send(behind1[:tokens], y=1), send(ahead1[tokens:], y=3)]
    piece2, *near, far10, far11, w00, w01 = tied((pieces[1], *near, *far1, *w0))
    far1, w0 = (far10, far11), (w00, w01)
    near = jnp.concatenate(near, axis=0)
    behind2, ahead2 = send(piece2, y=1), send(piece2, y=3)
    near_c = send(near, core=1)
    near_grads = joined(near, near_c)

    def with_near(total, steps):
        for step in range(4):
            if steps[step] is not None:
                total = total + contract(steps[step], near_grads[step])
        return total

    def begun(piece, ahead, behind):
        total = with_own([piece[:tokens], ahead[:tokens], None, behind[:tokens]])
        return with_near(total, [piece[tokens:], ahead[tokens:], None, behind[tokens:]])

    def ended(total, far):
        total = total + contract(far[0], grads[2]) + contract(far[1], near_grads[2])
        return total.reshape(4, BLOCK, width)

    total1 = begun(piece1, ahead1, behind1)
    total1 = ended(total1, far1)
    x1 = first_x(total1)
    sums0 = total0[:, 0] + w0[0] + w0[1]
    across0 = send(sums0[1], z=1)
    behind2, ahead2, across0, *x1 = tied((behind2, ahead2, across0, *x1))
    far2 = [send(behind2[:tokens], y=1), send(ahead2[tokens:], y=3)]
    w1 = second_x(total1, *x1)
    total2 = begun(piece2, ahead2, behind2)
    total2, *far2 = tied((total2, *far2))
    total2 = ended(total2, far2)
    x2 = first_x(total2)
    w10, w11, *x2 = tied((*w1, *x2))
    w1 = w10, w11
    w2 = second_x(total2, *x2)
    rows = [sums0[0] + across0] + [
        total[0] + w[0] + w[1] for total, w in ((total1, w1), (total2, w2))
    ]
    return jnp.concatenate(rows, axis=0)


def solution(mesh):
    return jax.shard_map(
        body,
        mesh=mesh,
        in_specs=(
            P(("dp", "tensor"), None),
            P(("dp", "tensor"), None),
            P("dp", "tensor"),
            P("dp", "tensor"),
        ),
        out_specs=P("dp", "tensor"),
        check_vma=False,
    )
```

```python
import jax
import jax.numpy as jnp
from jax import lax
from jax.experimental import pallas as pl
from jax.experimental.pallas import tpu as pltpu
from jax.sharding import PartitionSpec as P

AXES = ("dp", "tensor")
BLOCK = 128
STEPS = (0, 1, 3, 2)
PARTS = 3


def place(index):
    dp, tensor = index // 8, index % 8
    return dp // 4, tensor % 4, (tensor // 4) * 2 + (dp // 2) % 2, dp % 2


def index_of(x, y, z, core):
    return ((x * 2 + z % 2) * 2 + core) * 8 + (z // 2) * 4 + y


def send(value, x=0, y=0, z=0, core=0):
    pairs = []
    for source in range(128):
        sx, sy, sz, sc = place(source)
        pairs.append((source, index_of((sx + x) % 4, (sy + y) % 4, sz ^ z, sc ^ core)))
    return lax.ppermute(value, AXES, pairs)


def act_kernel(where, mant, scale, out):
    x, z_lo, core = where[0], where[1], where[2]
    for owner in range(16):
        ox, oz, oc = owner // 4, (owner // 2) % 2, owner % 2
        slot = lax.rem(ox - x + 4, 4)
        for k in range(PARTS):
            b = owner * PARTS + k
            values = mant[:, b * BLOCK : (b + 1) * BLOCK].astype(jnp.float32) * scale[:, b : b + 1]
            lanes = pl.ds(pl.multiple_of(slot * BLOCK, BLOCK), BLOCK)
            out[oc ^ core, oz ^ z_lo, k, :, lanes] = values.astype(jnp.bfloat16)


def widen_act(mant, exponent, where):
    tokens = mant.shape[0]
    return pl.pallas_call(
        act_kernel,
        out_shape=jax.ShapeDtypeStruct((2, 2, PARTS, tokens, 4 * BLOCK), jnp.bfloat16),
        in_specs=[
            pl.BlockSpec(memory_space=pltpu.SMEM),
            pl.BlockSpec(memory_space=pltpu.VMEM),
            pl.BlockSpec(memory_space=pltpu.VMEM),
        ],
        out_specs=pl.BlockSpec(memory_space=pltpu.VMEM),
        compiler_params=pltpu.CompilerParams(vmem_limit_bytes=8 * 1024 * 1024),
        cost_estimate=pl.CostEstimate(flops=0, bytes_accessed=8 * 1024 * 1024, transcendentals=0),
    )(where, mant, jnp.exp2(exponent.astype(jnp.float32)))


def grad_kernel(order, mant, scale, out):
    out[0] = (mant[...].astype(jnp.float32) * scale[0]).astype(jnp.bfloat16)


def widen_grad(mant, exponent, order):
    blocks, width = exponent.shape
    scale = jnp.exp2(exponent.astype(jnp.float32)).reshape(blocks, 1, width)
    return pl.pallas_call(
        grad_kernel,
        out_shape=jax.ShapeDtypeStruct((blocks, BLOCK, width), jnp.bfloat16),
        grid_spec=pltpu.PrefetchScalarGridSpec(
            num_scalar_prefetch=1,
            grid=(blocks,),
            in_specs=[
                pl.BlockSpec((BLOCK, width), lambda i, order: (order[i], 0)),
                pl.BlockSpec((1, 1, width), lambda i, order: (order[i], 0, 0)),
            ],
            out_specs=pl.BlockSpec((1, BLOCK, width), lambda i, order: (i, 0, 0)),
        ),
        compiler_params=pltpu.CompilerParams(vmem_limit_bytes=8 * 1024 * 1024),
        cost_estimate=pl.CostEstimate(flops=0, bytes_accessed=16 * 1024 * 1024, transcendentals=0),
    )(order, mant, scale)


def contract(left, right):
    return lax.dot_general(
        left, right, (((0,), (0,)), ((), ())), preferred_element_type=jnp.float32
    )


def tied(values, *others):
    return lax.optimization_barrier((*values, *others))[: len(values)]


def body(act_mant, act_exp, grad_mant, grad_exp):
    dp, tensor = lax.axis_index("dp"), lax.axis_index("tensor")
    x, z_lo, core = dp // 4, (dp // 2) % 2, dp % 2
    z_hi, y = tensor // 4, tensor % 4

    act = widen_act(act_mant, act_exp, jnp.stack([x, z_lo, core]).astype(jnp.int32))
    order = jnp.stack(
        [(z_hi ^ flip) * 4 + (y + step) % 4 for step in STEPS for flip in range(2)]
    ).astype(jnp.int32)
    other = send(act[1], core=1)
    (grad_mant,) = tied((grad_mant,), act)
    own = widen_grad(grad_mant, grad_exp, order).reshape(4, 2, BLOCK, -1)
    width = own.shape[-1]
    half = width // 2
    tokens = 4 * BLOCK

    def joined(first, second):
        return jnp.stack([first, second], axis=2).reshape(-1, tokens, width)

    def first_x(total):
        return send(total[..., 2, :, :half], x=1), send(total[..., 2, :, half:], x=3)

    def second_x(total, first, second):
        up, down = total[..., 1, :, :], total[..., 3, :, :]
        up = jnp.concatenate([up[..., :half] + first, up[..., half:]], axis=-1)
        down = jnp.concatenate([down[..., :half], down[..., half:] + second], axis=-1)
        return send(up, x=1), send(down, x=3)

    pair = jnp.concatenate([act[0, :, 0], other[:, 0]], axis=1)
    (for_core,) = tied((own,), other)
    own_c = send(for_core, core=1)
    pair_z = send(pair, z=2)
    behind0, ahead0 = [send(pair, y=1)], [send(pair, y=3)]
    pair_z, mine, other, *_ = tied((pair_z, act[0], other), own_c, *behind0, *ahead0)
    behind0, ahead0 = behind0 + [send(pair_z, y=1)], ahead0 + [send(pair_z, y=3)]

    def along_z(k, mine, other):
        here, there = (
            jnp.concatenate([mine[flip, k], other[flip, k]], axis=0) for flip in range(2)
        )
        return jnp.concatenate(
            [here, send(here, z=2), send(there, z=1), send(there, z=3)], axis=0
        )

    piece0, behind0, ahead0 = (
        jnp.concatenate(parts, axis=1) for parts in ([pair, pair_z], behind0, ahead0)
    )
    pair = jnp.concatenate([mine[:, 1], other[:, 1]], axis=1)
    piece1 = jnp.concatenate([pair, send(pair, z=2)], axis=1)
    behind0, ahead0, piece1, mine, other = tied((behind0, ahead0, piece1, mine, other))
    far0 = [send(behind0[0], y=1), send(ahead0[1], y=3)]
    piece2 = along_z(2, mine, other)
    piece1, piece2, for_z, *far0 = tied((piece1, piece2, own, *far0))
    behind1, ahead1 = send(piece1, y=1), send(piece1, y=3)
    near = [send(for_z[:1], z=1)]

    grads = joined(own, own_c)

    def with_own(steps):
        total = contract(steps[0], grads[0])
        for step in range(1, len(steps)):
            total = total + contract(steps[step], grads[step])
        return total

    def of_both(*steps):
        return jnp.stack(
            [with_own([part[i] for part in steps]) for i in range(2)]
        ).reshape(2, 4, BLOCK, width)

    total0 = of_both(piece0, ahead0, behind0, far0)
    x0 = first_x(total0)
    w0 = second_x(total0, *x0)
    behind1, ahead1, for_z, near0 = tied((behind1, ahead1, for_z, near[0]), *x0)
    far1 = [send(behind1[0], y=1), send(ahead1[1], y=3)]
    near1 = send(for_z[1:2], z=1)
    piece2, for_z, near0, near1, far10, far11, w00, w01 = tied(
        (piece2, for_z, near0, near1, *far1, *w0)
    )
    w0 = w00, w01
    behind2, ahead2 = send(piece2, y=1), send(piece2, y=3)
    near2 = send(for_z[2:], z=1)
    total1 = of_both(piece1, ahead1, behind1, [far10, far11])
    x1 = first_x(total1)
    w1 = second_x(total1, *x1)
    behind2, ahead2, near2 = tied((behind2, ahead2, near2), *x1)
    far2 = [send(behind2[:tokens], y=1), send(ahead2[tokens:], y=3)]
    near = jnp.concatenate([near0, near1, near2], axis=0)
    sums0 = total0[:, 0] + w0[0] + w0[1]
    for_across, near_c = tied((sums0[1], send(near, core=1)))
    across0 = send(for_across, z=1)
    near_grads = joined(near, near_c)
    steps = piece2, ahead2, behind2
    total2 = with_own([part[:tokens] for part in steps])
    for step in range(3):
        total2 = total2 + contract(steps[step][tokens:], near_grads[step])
    total2, far20, far21, across0 = tied((total2, *far2, across0))
    total2 = total2 + contract(far20, grads[3]) + contract(far21, near_grads[3])
    total2 = total2.reshape(4, BLOCK, width)
    x2 = first_x(total2)
    w10, w11, *x2 = tied((*w1, *x2))
    sums1 = total1[:, 0] + w10 + w11
    across1 = send(sums1[1], z=1)
    w2 = second_x(total2, *x2)
    rows = [sums0[0] + across0, sums1[0] + across1, total2[0] + w2[0] + w2[1]]
    return jnp.concatenate(rows, axis=0)


def solution(mesh):
    return jax.shard_map(
        body,
        mesh=mesh,
        in_specs=(
            P(("dp", "tensor"), None),
            P(("dp", "tensor"), None),
            P("dp", "tensor"),
            P("dp", "tensor"),
        ),
        out_specs=P("dp", "tensor"),
        check_vma=False,
    )
```
